256 devices in a mesh: grp: 4 (over z_hi, core), wide: 64 (over x, z_lo, y).
Axes of the slice: x: 4, y: 4, z: 8 (z_hi: 2, z_lo: 4; z = z_hi * 4 + z_lo), core: 2. Of those that a mesh axis runs over, the one named last changes fastest.
Arguments:
- samples: bfloat16 [4, 3072, 8, 1728], P('grp', 'wide')
- routes: int32 [4, 3072, 1], P('grp', 'wide'), may hold values from 0 to 63; in each aligned block of 48 rows (0 to 47, 48 to 95, ..., all dimensions but the last counted through in order) no two rows name the same one
- damping: float32 [64], P('wide'), may hold values from 0.25 to 4
Outputs:
- inv_root: float32 [64, 1728, 1728], P('wide', 'grp')
- scale: float32 [64], P('wide')
The draws below stay inside these ranges and needn't reach their ends.
Inputs may be any that keep to these rules, and one draw needn't show every extreme that they name: `routes`: in the 48 strips of one device, no factor is named by more than 1 strips; every factor is named by some strip.
All inputs are finite; a program needn't handle non-finite values.
Results may differ from the reference program's by a relative error of at most 0.0037.
Values may be sent and summed in bfloat16 or wider, within the bound.
A program may use at most 64 MiB of HBM per device.

```python
import math
import jax
import jax.numpy as jnp
import numpy as np
from jax import lax

W = 1728
STRIP = 8
SLOTS = 48
POWER = 6
MOST = 1
N_GRP = 4
N_WIDE = 64


def draw_samples(key, part):
    key = jax.random.fold_in(key, 11)
    key_scale, key_base = jax.random.split(key, 2)
    shape = (N_GRP, N_WIDE * SLOTS, STRIP, W)
    scales = jnp.exp(jax.random.uniform(key_scale, (W,), jnp.float32, 0.0, math.log(4.0)))
    values = jax.random.normal(key_base, shape, jnp.float32) * scales
    return values.astype(jnp.bfloat16)


def levels(stream_key, dims, pieces, least, largest):
    gain, own = 1.0, jax.random.fold_in(stream_key, 6)
    for position, parts in pieces:
        draws = jnp.exp(jax.random.uniform(jax.random.fold_in(own, position), (parts,), jnp.float32, least / len(pieces), largest / len(pieces)))
        gain = gain * jnp.repeat(draws, dims[position] // parts).reshape([-1 if axis == position else 1 for axis in range(len(dims))])
    return gain


def assign_block(key, own, number, rows, amount, top, reach, lean):
    order = jax.random.permutation(key, amount)
    crowded, ordinary = load_shares(amount, rows * top, reach, lean, True), load_shares(amount, rows * top, reach, lean, False)
    places = jnp.arange(amount)

    def named(sizes, offset_by):
        used = int((sizes > 0).sum())
        fixed = max(1, used // 4)
        shifted = fixed + (places - fixed + offset_by * (used - fixed)) % max(1, amount - fixed)
        return jnp.zeros((amount,), jnp.int32).at[order[jnp.where(places < fixed, places, shifted)]].set(jnp.asarray(sizes, jnp.int32))

    sizes = jnp.where(number % 4 == 0, named(crowded, number // 4), named(ordinary, number - number // 4 - 1))
    mixed = jax.random.permutation(jax.random.fold_in(own, 3), amount)
    source_of, taker = mixed[0:amount // 2 * 2:2], mixed[1:amount // 2 * 2:2]
    margin = jnp.minimum(sizes[source_of] - 1, reach - sizes[taker]) // 2
    margin = jnp.where((source_of == order[0]) | (taker == order[0]) | (sizes[taker] == 0), 0, jnp.maximum(margin, 0))
    shifted = jax.random.randint(jax.random.fold_in(own, 4), (amount // 2,), 0, 1 << 20) % (margin + 1)
    sizes = sizes.at[source_of].add(-shifted).at[taker].add(shifted)
    labels = jnp.searchsorted(jnp.cumsum(sizes), jnp.arange(rows * top), side="right").astype(jnp.int32)
    grid = labels.reshape(top, rows).T
    grid = grid[jax.random.permutation(jax.random.fold_in(own, 1), rows)]
    offset_by = jax.random.randint(jax.random.fold_in(own, 2), (rows, 1), 0, top)
    return jnp.take_along_axis(grid, (jnp.arange(top)[None, :] + offset_by) % top, axis=1)


def load_shares(number_of, total, most, lean, full):
    portions = [(1 << 20) // math.isqrt(grade ** lean) + 1 for grade in range(1, number_of + 1)]
    largest = most if full else min(most, max(-(-total // number_of), total * portions[0] // sum(portions)))
    least = 1 if total - largest >= number_of - 1 else 0
    counts, rest = [largest] + [least] * (number_of - 1), total - largest - least * (number_of - 1)
    while rest > 0:
        candidates = [i for i in range(1, number_of) if counts[i] < largest] or [i for i in range(1, number_of) if counts[i] < most]
        mass, left = sum([portions[i] for i in candidates]), rest
        for i in candidates:
            extra = min(most - counts[i], max(1, left * portions[i] // mass), rest)
            counts[i] = counts[i] + extra
            rest = rest - extra
    return np.array(counts)


def setup_inputs(seed: int = 0) -> dict:
    key_of = jax.random.split(jax.random.key(seed), 4)
    samples = draw_samples(jax.random.fold_in(key_of[3], 71), 0)
    routes_keys = jax.random.split(jax.random.fold_in(key_of[1], 1), N_GRP * (N_WIDE * SLOTS) // SLOTS)
    routes_turns = jax.random.permutation(jax.random.fold_in(key_of[1], 3), N_GRP * (N_WIDE * SLOTS) // SLOTS)
    routes = jax.vmap(lambda own, number: assign_block(jax.random.fold_in(key_of[1], 2), own, number, SLOTS, N_WIDE, 1, MOST, 2))(routes_keys, routes_turns).reshape((N_GRP, N_WIDE * SLOTS, 1))
    damping = jnp.clip(jnp.exp(math.log(4.0) - 2.7725887 * jax.random.uniform(key_of[2], (N_WIDE,), jnp.float32) ** levels(key_of[2], (N_WIDE,), ((0, 64),), -0.2, 0.2)), 0.25, 4.0)
    return {"samples": samples, "routes": routes, "damping": damping}


def reference(samples, routes, damping):
    nblocks = N_GRP * N_WIDE
    blocks = samples.reshape(nblocks, SLOTS, STRIP, W)
    dest = routes.reshape(nblocks, SLOTS)
    eye = jnp.eye(W, dtype=jnp.float32)
    slot_ids = jnp.arange(SLOTS, dtype=jnp.int32)
    rank_ids = jnp.arange(MOST, dtype=jnp.int32)

    def one_factor(args):
        factor_id, damp = args
        hit = (dest == factor_id).astype(jnp.int32)
        rank = jnp.cumsum(hit, 1) - hit
        pick = hit[:, :, None] * (rank[:, :, None] == rank_ids[None, None, :]).astype(jnp.int32)
        index = lax.optimization_barrier(jnp.sum(pick * slot_ids[None, :, None], 1)).astype(jnp.int32)
        valid = lax.optimization_barrier(jnp.sum(pick, 1))
        chosen = jnp.take_along_axis(blocks, index[:, :, None, None], axis=1)
        chosen = chosen * valid[:, :, None, None].astype(jnp.bfloat16)
        stacked = chosen.reshape(nblocks * MOST * STRIP, W)
        gram = lax.dot_general(stacked, stacked, (((0,), (0,)), ((), ())), preferred_element_type=jnp.float32)
        nrows = STRIP * jnp.sum(hit).astype(jnp.float32)
        shift = damp * jnp.trace(gram) / (nrows * W)
        factor = gram / nrows + shift * eye
        vector = jnp.full((W,), 1.0 / math.sqrt(W), jnp.float32)
        estimate = jnp.float32(0.0)
        for turn in range(POWER):
            image = jnp.dot(factor, vector, precision=lax.Precision.HIGHEST)
            estimate = jnp.sum(vector * image)
            vector = image / jnp.sqrt(jnp.sum(image * image))
        bound = 1.1 * estimate
        y0 = (factor / bound).astype(jnp.bfloat16)
        t0 = ((3.0 * eye - y0.astype(jnp.float32)) * 0.5).astype(jnp.bfloat16)
        y1 = jnp.dot(y0, t0, preferred_element_type=jnp.float32).astype(jnp.bfloat16)
        m1 = jnp.dot(t0, y1, preferred_element_type=jnp.float32)
        t1 = ((3.0 * eye - m1) * 0.5).astype(jnp.bfloat16)
        z2 = jnp.dot(t1, t0, preferred_element_type=jnp.float32)
        return (z2, bound)
    inv_root, scale = lax.map(one_factor, (jnp.arange(N_WIDE, dtype=jnp.int32), damping))
    return (inv_root, scale)
```

```python
import functools
import math

import jax
import jax.numpy as jnp
from jax import lax
from jax.experimental import pallas as pl
from jax.experimental.pallas import tpu as pltpu
from jax.sharding import PartitionSpec as P

POWER = 6
MESH = pl.DeviceIdType.MESH
F32, BF16 = jnp.float32, jnp.bfloat16
LANES = 128
TILE = 256

STEPS = (
    (0, 0), (1, 0), (1, 1), (3, 0), (3, 3), (0, 1), (1, 3), (0, 3),
    (3, 1), (2, 1), (2, 0), (1, 2), (0, 2), (2, 3), (2, 2), (3, 2),
)
LAG = 6


def device(z, core, x, y):
    return (lax.div(z, 4) * 2 + core, x * 16 + lax.rem(z, 4) * 4 + y)


def fused(width, strip, ext, routes, damping, out, scale, sib_out, sib_in, own, cells, staged, stack, gram, y_all, t_all, t_rows, a_rows, t_next, column, sib_send, sib_recv, plane_send, plane_recv, z_send, group_recv, pass_send, pass_recv):
    member, worker = lax.axis_index("grp"), lax.axis_index("wide")
    core = lax.rem(member, 2)
    x, y = lax.div(worker, 16), lax.rem(worker, 4)
    z = lax.div(member, 2) * 4 + lax.rem(lax.div(worker, 4), 4)
    place = x * 4 + y
    even = lax.rem(z, 2) == core
    wide = ext.shape[1]
    tiles = wide // TILE
    rows = out.shape[0]
    pair_rows = 2 * strip

    def peer(dx, dy):
        return lax.rem(x + dx, 4), lax.rem(y + dy, 4)

    barrier = pltpu.get_barrier_semaphore()
    pl.semaphore_signal(barrier, inc=1, device_id=device(z, 1 - core, x, y), device_id_type=MESH)
    for dx, dy in STEPS[1:]:
        px, py = peer(dx, dy)
        pl.semaphore_signal(barrier, inc=1, device_id=device(z, core, px, py), device_id_type=MESH)
    for dz in range(1, 8):
        pl.semaphore_signal(barrier, inc=1, device_id=device(lax.rem(z + dz, 8), lax.rem(z, 2), x, y), device_id_type=MESH)

    def choose(parity):
        shape = (16 * pair_rows, ext.shape[0])
        row = lax.broadcasted_iota(jnp.int32, shape, 0)
        col = lax.broadcasted_iota(jnp.int32, shape, 1)
        where = row // pair_rows
        plane = 2 * ((row // strip) % 2) + parity
        factor = (where // 4) * 16 + plane * 4 + where % 4
        hit = (routes[...] == factor) & (row % strip == col % strip)
        pick = jnp.where(hit, 1.0, 0.0).astype(BF16)
        chosen = jnp.dot(pick, ext[...], preferred_element_type=F32)
        return chosen.astype(BF16).reshape(16, pair_rows, wide)

    sib_out[...] = choose(1 - core)
    pl.semaphore_wait(barrier, jnp.where(even, 22, 24))
    sibling = device(z, 1 - core, x, y)

    def sib_copy(step):
        px, py = peer(*STEPS[step])
        at = px * 4 + py
        return pltpu.make_async_remote_copy(
            sib_out.at[at], sib_in.at[at], sib_send.at[step], sib_recv.at[step], device_id=sibling, device_id_type=MESH
        )

    for step in range(16):
        sib_copy(step).start()
    own[...] = choose(core)

    def plane_copy(step):
        px, py = peer(*STEPS[step])
        return pltpu.make_async_remote_copy(
            cells.at[pl.ds(2 * (px * 4 + py), 2)],
            staged.at[pl.ds(2 * place, 2)],
            plane_send.at[step],
            plane_recv.at[step],
            device_id=device(z, core, px, py),
            device_id_type=MESH,
        )

    for step in range(16):
        px, py = peer(*STEPS[step])
        at = px * 4 + py
        sib_copy(step).wait_recv()
        mine, other = own[at].astype(F32), sib_in[at].astype(F32)
        for j in range(2):
            part = slice(j * strip, (j + 1) * strip)
            cells[2 * at + j] = jnp.concatenate([mine[part], other[part]], 0).astype(BF16)
        if step > 0:
            plane_copy(step).start()

    def origin(step):
        dx, dy = STEPS[step]
        return peer(4 - dx, 4 - dy)

    def z_copy(step, dz, slot, near=False):
        sx, sy = origin(step)
        target = lax.rem(z + dz, 8)
        j = lax.div(lax.rem(target, 4), 2)
        source = cells if step == 0 else staged
        cell = source.at[2 * (sx * 4 + sy) + j]
        landing = stack.at[step * 8 + z]
        if near:
            return pltpu.make_async_copy(cell, landing, group_recv.at[step])
        return pltpu.make_async_remote_copy(
            cell,
            landing,
            z_send.at[step, slot],
            group_recv.at[step],
            device_id=device(target, lax.rem(sx + sy, 2), x, y),
            device_id_type=MESH,
        )

    def direct(step):
        sx, sy = origin(step)
        return lax.rem(sx + sy, 2) == core

    def z_start(step):
        if step > 0:
            plane_copy(step).wait_recv()

        @pl.when(even)
        def _():
            for slot, dz in enumerate((4, 2, 6)):
                z_copy(step, dz, slot).start()

            @pl.when(direct(step))
            def _():
                z_copy(step, 0, 3, near=True).start()

            @pl.when(jnp.logical_not(direct(step)))
            def _():
                z_copy(step, 0, 3).start()

        @pl.when(jnp.logical_not(even))
        def _():
            for slot, dz in enumerate((5, 3, 1, 7)):
                z_copy(step, dz, slot).start()

    def z_finish(step):
        for slot in range(3):
            z_copy(step, 1, slot).wait_send()

        @pl.when(jnp.logical_not(even & direct(step)))
        def _():
            z_copy(step, 1, 3).wait_send()

    def pass_copy(step):
        group = stack.at[pl.ds(step * 8, 8)]
        return pltpu.make_async_remote_copy(
            group, group, pass_send.at[step], pass_recv.at[step], device_id=sibling, device_id_type=MESH
        )

    def arrive(pair):
        for step in (2 * pair, 2 * pair + 1):
            group = stack.at[pl.ds(step * 8, 8)]

            @pl.when(direct(step))
            def _():
                pltpu.make_async_copy(group, group, group_recv.at[step]).wait()
                pass_copy(step).start()

        for step in (2 * pair, 2 * pair + 1):

            @pl.when(jnp.logical_not(direct(step)))
            def _():
                pass_copy(step).wait_recv()

    depth = 16 * pair_rows

    def accumulate(pair):
        block = stack[pl.ds(pair * 16, 16)].reshape(depth, wide)

        def body(i, _):
            left = stack[pl.ds(pair * 16, 16), :, pl.ds(pl.multiple_of(i * TILE, TILE), TILE)].reshape(depth, TILE)
            term = lax.dot_general(left, block, (((0,), (0,)), ((), ())), preferred_element_type=F32)
            at = pl.ds(pl.multiple_of(i * TILE, TILE), TILE)
            if pair == 0:
                gram[at, :] = term
            else:
                gram[at, :] += term
            return 0

        lax.fori_loop(0, tiles, body, 0)

    for turn in range(8 + LAG // 2):
        if turn < 8:
            z_start(2 * turn)
            z_start(2 * turn + 1)
        if turn >= LAG // 2:
            arrive(turn - LAG // 2)
            accumulate(turn - LAG // 2)

    eye = (
        lax.broadcasted_iota(jnp.int32, (LANES, LANES), 0) == lax.broadcasted_iota(jnp.int32, (LANES, LANES), 1)
    ).astype(F32)
    last = wide - LANES
    inside = lax.broadcasted_iota(jnp.int32, (1, LANES), 1) < width - last
    lane = lax.broadcasted_iota(jnp.int32, (1, LANES), 1)
    count = jnp.sum(jnp.where(lane == width - last, gram[pl.ds(width, 8), pl.ds(last, LANES)][0:1], 0.0))

    def clear(i, _):
        at = pl.ds(pl.multiple_of(i * TILE, TILE), TILE)
        gram[at, pl.ds(last, LANES)] = jnp.where(inside, gram[at, pl.ds(last, LANES)], 0.0)
        return 0

    lax.fori_loop(0, tiles, clear, 0)
    gram[pl.ds(width, wide - width), :] = jnp.zeros((wide - width, wide), F32)
    diagonal = jnp.zeros((LANES, LANES), F32)
    for b in range(wide // LANES):
        diagonal += gram[b * LANES : (b + 1) * LANES, b * LANES : (b + 1) * LANES] * eye
    trace = jnp.sum(diagonal)
    lift = damping[0] * trace / width
    unit = width / trace
    for b in range(wide // LANES):
        at = slice(b * LANES, (b + 1) * LANES)
        gram[at, at] += lift * (eye if b < wide // LANES - 1 else jnp.where(inside, eye, 0.0))

    chunk = 64

    def to_column(row, factor):
        def body(i, _):
            at = pl.ds(pl.multiple_of(i * chunk, chunk), chunk)
            total = jnp.sum(gram[at, :] * row, axis=1, keepdims=True) * factor
            column[at, :] = jnp.broadcast_to(total, (chunk, LANES))
            return 0

        lax.fori_loop(0, wide // chunk, body, 0)

    def to_row(factor):
        def body(i, sums):
            at = pl.ds(pl.multiple_of(i * chunk, chunk), chunk)
            value = column[at, :]
            return tuple(
                part + jnp.sum((gram[at, b * LANES : (b + 1) * LANES] * value).reshape(chunk // 8, 8, LANES), axis=0)
                for b, part in enumerate(sums)
            )

        sums = lax.fori_loop(0, wide // chunk, body, tuple(jnp.zeros((8, LANES), F32) for _ in range(wide // LANES)))
        return jnp.concatenate([jnp.sum(part, axis=0, keepdims=True) for part in sums], axis=1) * factor

    lane_all = lax.broadcasted_iota(jnp.int32, (1, wide), 1)
    vector = jnp.where(lane_all < width, 1.0 / math.sqrt(width), 0.0).astype(F32)
    to_column(vector, unit)
    vector = to_row(unit)
    to_column(vector, unit)
    norm = jnp.sum(column[...] * column[...]) * (1.0 / LANES)
    vector = to_row(unit * lax.rsqrt(norm))
    to_column(vector, unit)
    fifth = jnp.concatenate(
        [jnp.sum(column[b * LANES : (b + 1) * LANES, :] * eye, axis=0, keepdims=True) for b in range(wide // LANES)], axis=1
    )
    sixth = to_row(unit)
    bound = 1.1 * (jnp.sum(fifth * sixth) / jnp.sum(fifth * fifth))
    scale[0, 0] = bound * (trace / (count * width))
    rate = unit / bound

    def normalize(i, _):
        at = pl.ds(pl.multiple_of(i * LANES, LANES), LANES)
        y_part = (gram[at, :] * rate).astype(BF16)
        row = lax.broadcasted_iota(jnp.int32, (LANES, wide), 0) + i * LANES
        col = lax.broadcasted_iota(jnp.int32, (LANES, wide), 1)
        three = jnp.where((row == col) & (col < width), 3.0, 0.0)
        y_all[at, :] = y_part
        t_all[at, :] = ((three - y_part.astype(F32)) * 0.5).astype(BF16)
        return 0

    lax.fori_loop(0, wide // LANES, normalize, 0)

    first = member * rows
    t_rows[...] = t_all[pl.ds(pl.multiple_of(first, 16), rows), :]

    def step_one(i, _):
        at = pl.ds(pl.multiple_of(i * TILE, TILE), TILE)
        a_rows[:, at] = jnp.dot(t_rows[...], y_all[:, at], preferred_element_type=F32).astype(BF16)
        return 0

    lax.fori_loop(0, tiles, step_one, 0)

    def step_two(i, _):
        at = pl.ds(pl.multiple_of(i * TILE, TILE), TILE)
        m_part = jnp.dot(a_rows[...], t_all[:, at], preferred_element_type=F32)
        row = lax.broadcasted_iota(jnp.int32, (rows, TILE), 0) + first
        col = lax.broadcasted_iota(jnp.int32, (rows, TILE), 1) + i * TILE
        three = jnp.where(row == col, 3.0, 0.0)
        t_next[:, at] = ((three - m_part) * 0.5).astype(BF16)
        return 0

    lax.fori_loop(0, tiles, step_two, 0)

    def step_three(i, _):
        at = pl.ds(pl.multiple_of(i * TILE, TILE), TILE)
        out[:, at] = jnp.dot(t_next[...], t_all[:, at], preferred_element_type=F32)
        return 0

    lax.fori_loop(0, tiles - 1, step_three, 0)
    tail = (tiles - 1) * TILE
    out[:, tail:width] = jnp.dot(t_next[...], t_all[:, tail:], preferred_element_type=F32)[:, : width - tail]

    for step in range(16):
        sib_copy(step).wait_send()
        if step > 0:
            plane_copy(step).wait_send()
        z_finish(step)

        @pl.when(direct(step))
        def _():
            pass_copy(step).wait_send()


def per_device(samples, routes, damping):
    members = lax.axis_size("grp")
    _, slots, strip, width = samples.shape
    wide = -(-width // TILE) * TILE
    rows = width // members
    strips = samples[0].reshape(slots * strip, width)
    mark = (lax.broadcasted_iota(jnp.int32, (slots * strip, wide - width), 1) == 0).astype(BF16)
    ext = jnp.concatenate([strips, mark], axis=1)
    named = jnp.repeat(routes[0, :, 0], strip)[None]
    vmem = pl.BlockSpec(memory_space=pltpu.VMEM)
    smem = pl.BlockSpec(memory_space=pltpu.SMEM)
    dma = pltpu.SemaphoreType.DMA
    result, scale = pl.pallas_call(
        functools.partial(fused, width, strip),
        out_shape=(jax.ShapeDtypeStruct((rows, width), F32), jax.ShapeDtypeStruct((1, 1), F32)),
        in_specs=[vmem, vmem, smem],
        out_specs=(vmem, smem),
        scratch_shapes=[
            pltpu.VMEM((16, 2 * strip, wide), BF16),
            pltpu.VMEM((16, 2 * strip, wide), BF16),
            pltpu.VMEM((16, 2 * strip, wide), BF16),
            pltpu.VMEM((32, 2 * strip, wide), BF16),
            pltpu.VMEM((32, 2 * strip, wide), BF16),
            pltpu.VMEM((128, 2 * strip, wide), BF16),
            pltpu.VMEM((wide, wide), F32),
            pltpu.VMEM((wide, wide), BF16),
            pltpu.VMEM((wide, wide), BF16),
            pltpu.VMEM((rows, wide), BF16),
            pltpu.VMEM((rows, wide), BF16),
            pltpu.VMEM((rows, wide), BF16),
            pltpu.VMEM((wide, LANES), F32),
            dma((16,)),
            dma((16,)),
            dma((16,)),
            dma((16,)),
            dma((16, 4)),
            dma((16,)),
            dma((16,)),
            dma((16,)),
        ],
        compiler_params=pltpu.CompilerParams(
            collective_id=0, has_side_effects=True, vmem_limit_bytes=60 * 1024 * 1024
        ),
        name="inverse_root",
    )(ext, named, damping)
    return (result[None], scale.reshape(1))


def solution(mesh):
    in_specs = (P("grp", "wide", None, None), P("grp", "wide", None), P("wide"))
    out_specs = (P("wide", "grp", None), P("wide"))
    return jax.shard_map(
        per_device, mesh=mesh, in_specs=in_specs, out_specs=out_specs, check_vma=False
    )
```

```python
import functools
import math

import jax
import jax.numpy as jnp
from jax import lax
from jax.experimental import pallas as pl
from jax.experimental.pallas import tpu as pltpu
from jax.sharding import PartitionSpec as P

POWER = 6
MESH = pl.DeviceIdType.MESH
F32, BF16 = jnp.float32, jnp.bfloat16
LANES = 128
TILE = 256

STEPS = (
    (0, 0), (1, 0), (1, 1), (3, 0), (3, 3), (0, 1), (1, 3), (0, 3),
    (3, 1), (2, 1), (2, 0), (1, 2), (0, 2), (2, 3), (2, 2), (3, 2),
)
LAG = 6


def device(z, core, x, y):
    return (lax.div(z, 4) * 2 + core, x * 16 + lax.rem(z, 4) * 4 + y)


def fused(width, strip, slots, strips, routes, damping, out, scale, ext, chosen, staged, cells, stack, gram, t_all, t_rows, a_rows, t_next, vectors, plane_send, plane_recv, z_send, group_recv, pass_send, pass_recv):
    member, worker = lax.axis_index("grp"), lax.axis_index("wide")
    core = lax.rem(member, 2)
    x, y = lax.div(worker, 16), lax.rem(worker, 4)
    z = lax.div(member, 2) * 4 + lax.rem(lax.div(worker, 4), 4)
    even = lax.rem(z, 2) == core
    wide = ext.shape[1]
    tiles = wide // TILE
    rows = out.shape[0]
    pair_rows = 2 * strip
    last = wide - LANES

    def peer(dx, dy):
        return lax.rem(x + dx, 4), lax.rem(y + dy, 4)

    barrier = pltpu.get_barrier_semaphore()
    pl.semaphore_signal(barrier, inc=1, device_id=device(z, 1 - core, x, y), device_id_type=MESH)
    for dx, dy in STEPS[1:]:
        px, py = peer(dx, dy)
        for there in range(2):
            pl.semaphore_signal(barrier, inc=1, device_id=device(z, there, px, py), device_id_type=MESH)
    for dz in range(1, 8):
        pl.semaphore_signal(barrier, inc=1, device_id=device(lax.rem(z + dz, 8), lax.rem(z, 2), x, y), device_id_type=MESH)

    ext[:, :last] = strips[:, :last]
    mark = lax.broadcasted_iota(jnp.int32, (slots * strip, wide - width), 1) == 0
    ext[:, last:] = jnp.concatenate([strips[:, last:].astype(F32), jnp.where(mark, 1.0, 0.0)], axis=1).astype(BF16)
    spread = lax.broadcasted_iota(jnp.int32, (slots, slots * strip), 1) // strip == lax.broadcasted_iota(
        jnp.int32, (slots, slots * strip), 0
    )
    named = jnp.broadcast_to(routes[...].astype(F32), (8, slots)).astype(BF16)
    named = jnp.dot(named, jnp.where(spread, 1.0, 0.0).astype(BF16), preferred_element_type=F32)[0:1].astype(jnp.int32)
    shape = (32 * pair_rows, slots * strip)
    row = lax.broadcasted_iota(jnp.int32, shape, 0)
    col = lax.broadcasted_iota(jnp.int32, shape, 1)
    place, plane = row // (2 * pair_rows), 2 * ((row // strip) % 2) + (row // pair_rows) % 2
    factor = (place // 4) * 16 + plane * 4 + place % 4
    pick = jnp.where((named == factor) & (row % strip == col % strip), 1.0, 0.0).astype(BF16)
    chosen[...] = jnp.dot(pick, ext[...], preferred_element_type=F32).astype(BF16).reshape(32, pair_rows, wide)
    pl.semaphore_wait(barrier, jnp.where(even, 37, 39))

    def plane_copy(step, there):
        px, py = peer(*STEPS[step])
        return pltpu.make_async_remote_copy(
            chosen.at[2 * (px * 4 + py) + there],
            staged.at[2 * step + core],
            plane_send.at[step, there],
            plane_recv.at[step, core],
            device_id=device(z, there, px, py),
            device_id_type=MESH,
        )

    def plane_each(step, act):
        for there in range(2):
            if step > 0:
                act(plane_copy(step, there))
            else:

                @pl.when(core != there)
                def _():
                    act(plane_copy(step, there))

    def plane_wait(step):
        for source in range(2):
            landed = staged.at[2 * step + source]
            if step > 0:
                pltpu.make_async_copy(landed, landed, plane_recv.at[step, source]).wait()
            else:

                @pl.when(core != source)
                def _():
                    pltpu.make_async_copy(landed, landed, plane_recv.at[step, source]).wait()

    for step in range(16):
        plane_each(step, lambda copy: copy.start())
    staged[core] = chosen[2 * (x * 4 + y) + core]

    def origin(step):
        dx, dy = STEPS[step]
        return peer(4 - dx, 4 - dy)

    def direct(step):
        sx, sy = origin(step)
        return lax.rem(sx + sy, 2) == core

    def z_copy(step, dz, slot, near=False):
        sx, sy = origin(step)
        target = lax.rem(z + dz, 8)
        cell = cells.at[2 * step + lax.div(lax.rem(target, 4), 2)]
        landing = stack.at[step * 8 + z]
        if near:
            return pltpu.make_async_copy(cell, landing, group_recv.at[step])
        return pltpu.make_async_remote_copy(
            cell,
            landing,
            z_send.at[step, slot],
            group_recv.at[step],
            device_id=device(target, lax.rem(sx + sy, 2), x, y),
            device_id_type=MESH,
        )

    def z_start(step):
        plane_wait(step)
        one, two = staged[2 * step].astype(F32), staged[2 * step + 1].astype(F32)
        for j in range(2):
            part = slice(j * strip, (j + 1) * strip)
            cells[2 * step + j] = jnp.concatenate([one[part], two[part]], 0).astype(BF16)

        @pl.when(even)
        def _():
            for slot, dz in enumerate((4, 2, 6)):
                z_copy(step, dz, slot).start()

            @pl.when(direct(step))
            def _():
                z_copy(step, 0, 3, near=True).start()

            @pl.when(jnp.logical_not(direct(step)))
            def _():
                z_copy(step, 0, 3).start()

        @pl.when(jnp.logical_not(even))
        def _():
            for slot, dz in enumerate((5, 3, 1, 7)):
                z_copy(step, dz, slot).start()

    def z_finish(step):
        for slot in range(3):
            z_copy(step, 1, slot).wait_send()

        @pl.when(jnp.logical_not(even & direct(step)))
        def _():
            z_copy(step, 1, 3).wait_send()

    sibling = device(z, 1 - core, x, y)

    def pass_copy(step):
        group = stack.at[pl.ds(step * 8, 8)]
        return pltpu.make_async_remote_copy(
            group, group, pass_send.at[step], pass_recv.at[step], device_id=sibling, device_id_type=MESH
        )

    def arrive(pair):
        for step in (2 * pair, 2 * pair + 1):
            group = stack.at[pl.ds(step * 8, 8)]

            @pl.when(direct(step))
            def _():
                pltpu.make_async_copy(group, group, group_recv.at[step]).wait()
                pass_copy(step).start()

        for step in (2 * pair, 2 * pair + 1):

            @pl.when(jnp.logical_not(direct(step)))
            def _():
                pass_copy(step).wait_recv()

    depth, half = 16 * pair_rows, wide // 2

    def accumulate(pair):
        def body(i, _):
            at = pl.ds(pl.multiple_of(i * half, LANES), half)
            left = stack[pl.ds(pair * 16, 16), :, at].reshape(depth, half)
            block = stack[pl.ds(pair * 16, 16)].reshape(depth, wide)
            term = lax.dot_general(left, block, (((0,), (0,)), ((), ())), preferred_element_type=F32)
            if pair == 0:
                gram[at, :] = term
            else:
                gram[at, :] += term
            return 0

        lax.fori_loop(0, 2, body, 0)

    for turn in range(8 + LAG // 2):
        if turn < 8:
            z_start(2 * turn)
            z_start(2 * turn + 1)
        if turn >= LAG // 2:
            arrive(turn - LAG // 2)
            accumulate(turn - LAG // 2)

    eye = (
        lax.broadcasted_iota(jnp.int32, (LANES, LANES), 0) == lax.broadcasted_iota(jnp.int32, (LANES, LANES), 1)
    ).astype(F32)
    inside = lax.broadcasted_iota(jnp.int32, (1, LANES), 1) < width - last
    lane = lax.broadcasted_iota(jnp.int32, (1, LANES), 1)
    count = jnp.sum(jnp.where(lane == width - last, gram[pl.ds(width, 8), pl.ds(last, LANES)][0:1], 0.0))

    def clear(i, _):
        at = pl.ds(pl.multiple_of(i * TILE, TILE), TILE)
        gram[at, pl.ds(last, LANES)] = jnp.where(inside, gram[at, pl.ds(last, LANES)], 0.0)
        return 0

    lax.fori_loop(0, tiles, clear, 0)
    gram[pl.ds(width, wide - width), :] = jnp.zeros((wide - width, wide), F32)
    diagonal = jnp.zeros((LANES, LANES), F32)
    for b in range(wide // LANES):
        diagonal += gram[b * LANES : (b + 1) * LANES, b * LANES : (b + 1) * LANES] * eye
    trace = jnp.sum(diagonal)
    lift = damping[0] * trace / width
    unit = width / trace
    for b in range(wide // LANES):
        at = slice(b * LANES, (b + 1) * LANES)
        gram[at, at] += lift * (eye if b < wide // LANES - 1 else jnp.where(inside, eye, 0.0))

    blocks = wide // LANES

    def multiply(_, carry):
        factors = [vectors[1, :, b * LANES : (b + 1) * LANES] for b in range(blocks)]
        vectors[0] = vectors[1]
        for i in range(blocks):
            parts = []
            for q in range(LANES // 8):
                at = slice(i * LANES + q * 8, i * LANES + q * 8 + 8)
                total = gram[at, :LANES] * factors[0]
                for b in range(1, blocks):
                    total += gram[at, b * LANES : (b + 1) * LANES] * factors[b]
                parts.append(total)
            total = jnp.sum(jnp.concatenate(parts, axis=0).T, axis=0, keepdims=True) * unit
            vectors[1, :, i * LANES : (i + 1) * LANES] = jnp.broadcast_to(total, (8, LANES))
        return carry

    def half_turns(_, carry):
        lax.fori_loop(0, POWER // 2, multiply, 0)
        size = lax.rsqrt(jnp.sum(vectors[1] * vectors[1]) * 0.125)
        vectors[...] = vectors[...] * size
        return carry

    lane_all = lax.broadcasted_iota(jnp.int32, (8, wide), 1)
    vectors[1] = jnp.where(lane_all < width, 1.0 / math.sqrt(width), 0.0).astype(F32)
    lax.fori_loop(0, 2, half_turns, 0)
    before, vector = vectors[0], vectors[1]
    bound = 1.1 * (jnp.sum(before * vector) / jnp.sum(before * before))
    scale[0, 0] = bound * (trace / (count * width))
    rate = unit / bound

    def normalize(i, _):
        at = pl.ds(pl.multiple_of(i * LANES, LANES), LANES)
        t_all[at, :] = (gram[at, :] * (-0.5 * rate)).astype(BF16)
        return 0

    lax.fori_loop(0, blocks, normalize, 0)
    parts = []
    for b in range(blocks):
        at = slice(b * LANES, (b + 1) * LANES)
        ones = eye if b < blocks - 1 else jnp.where(inside, eye, 0.0)
        y_part = (gram[at, at] * rate).astype(BF16).astype(F32)
        t_part = ((3.0 * ones - y_part) * 0.5).astype(BF16)
        t_all[at, at] = t_part
        parts.append(jnp.sum((y_part + 2.0 * t_part.astype(F32)) * eye, axis=0, keepdims=True))
    lift_back = jnp.concatenate(parts, axis=1)

    first = member * rows
    t_rows[...] = t_all[pl.ds(pl.multiple_of(first, 16), rows), :]
    square = jnp.dot(t_rows[...], t_all[...], preferred_element_type=F32)
    a_rows[...] = (t_rows[...].astype(F32) * lift_back - 2.0 * square).astype(BF16)
    m_rows = jnp.dot(a_rows[...], t_all[...], preferred_element_type=F32)
    row = lax.broadcasted_iota(jnp.int32, (rows, wide), 0) + first
    col = lax.broadcasted_iota(jnp.int32, (rows, wide), 1)
    t_next[...] = (jnp.where(row == col, 1.5, 0.0) - 0.5 * m_rows).astype(BF16)
    out[...] = jnp.dot(t_next[...], t_all[...], preferred_element_type=F32)[:, :width]

    for step in range(16):
        plane_each(step, lambda copy: copy.wait_send())
        z_finish(step)

        @pl.when(direct(step))
        def _():
            pass_copy(step).wait_send()


def per_device(samples, routes, damping):
    members = lax.axis_size("grp")
    _, slots, strip, width = samples.shape
    wide = -(-width // TILE) * TILE
    rows = width // members
    vmem = pl.BlockSpec(memory_space=pltpu.VMEM)
    smem = pl.BlockSpec(memory_space=pltpu.SMEM)
    dma = pltpu.SemaphoreType.DMA
    result, scale = pl.pallas_call(
        functools.partial(fused, width, strip, slots),
        out_shape=(jax.ShapeDtypeStruct((rows, width), F32), jax.ShapeDtypeStruct((1, 1), F32)),
        in_specs=[vmem, vmem, smem],
        out_specs=(vmem, smem),
        scratch_shapes=[
            pltpu.VMEM((slots * strip, wide), BF16),
            pltpu.VMEM((32, 2 * strip, wide), BF16),
            pltpu.VMEM((32, 2 * strip, wide), BF16),
            pltpu.VMEM((32, 2 * strip, wide), BF16),
            pltpu.VMEM((128, 2 * strip, wide), BF16),
            pltpu.VMEM((wide, wide), F32),
            pltpu.VMEM((wide, wide), BF16),
            pltpu.VMEM((rows, wide), BF16),
            pltpu.VMEM((rows, wide), BF16),
            pltpu.VMEM((rows, wide), BF16),
            pltpu.VMEM((2, 8, wide), F32),
            dma((16, 2)),
            dma((16, 2)),
            dma((16, 4)),
            dma((16,)),
            dma((16,)),
            dma((16,)),
        ],
        compiler_params=pltpu.CompilerParams(
            collective_id=0, has_side_effects=True, vmem_limit_bytes=60 * 1024 * 1024
        ),
        name="inverse_root",
    )(samples.reshape(slots * strip, width), routes.reshape(1, slots), damping)
    return (result[None], scale.reshape(1))


def solution(mesh):
    in_specs = (P("grp", "wide", None, None), P("grp", "wide", None), P("wide"))
    out_specs = (P("wide", "grp", None), P("wide"))
    return jax.shard_map(
        per_device, mesh=mesh, in_specs=in_specs, out_specs=out_specs, check_vma=False
    )
```

```python
import functools
import math

import jax
import jax.numpy as jnp
from jax import lax
from jax.experimental import pallas as pl
from jax.experimental.pallas import tpu as pltpu
from jax.sharding import PartitionSpec as P

POWER = 6
MESH = pl.DeviceIdType.MESH
F32, BF16 = jnp.float32, jnp.bfloat16
LANES = 128
TILE = 256

STEPS = (
    (0, 0), (1, 0), (1, 1), (3, 0), (3, 3), (0, 1), (1, 3), (0, 3),
    (3, 1), (2, 1), (2, 0), (1, 2), (0, 2), (2, 3), (2, 2), (3, 2),
)
LAG = 6


def device(z, core, x, y):
    return (lax.div(z, 4) * 2 + core, x * 16 + lax.rem(z, 4) * 4 + y)


def collect(width, strip, slots, strips, routes, damping, gram, stats, ext, chosen, staged, cells, stack, plane_send, plane_recv, z_send, group_recv, pass_send, pass_recv):
    member, worker = lax.axis_index("grp"), lax.axis_index("wide")
    core = lax.rem(member, 2)
    x, y = lax.div(worker, 16), lax.rem(worker, 4)
    z = lax.div(member, 2) * 4 + lax.rem(lax.div(worker, 4), 4)
    even = lax.rem(z, 2) == core
    wide = ext.shape[1]
    tiles = wide // TILE
    pair_rows = 2 * strip
    last = wide - LANES

    def peer(dx, dy):
        return lax.rem(x + dx, 4), lax.rem(y + dy, 4)

    barrier = pltpu.get_barrier_semaphore()
    pl.semaphore_signal(barrier, inc=1, device_id=device(z, 1 - core, x, y), device_id_type=MESH)
    for dx, dy in STEPS[1:]:
        px, py = peer(dx, dy)
        for there in range(2):
            pl.semaphore_signal(barrier, inc=1, device_id=device(z, there, px, py), device_id_type=MESH)
    for dz in range(1, 8):
        pl.semaphore_signal(barrier, inc=1, device_id=device(lax.rem(z + dz, 8), lax.rem(z, 2), x, y), device_id_type=MESH)

    ext[:, :last] = strips[:, :last]
    mark = lax.broadcasted_iota(jnp.int32, (slots * strip, wide - width), 1) == 0
    ext[:, last:] = jnp.concatenate([strips[:, last:].astype(F32), jnp.where(mark, 1.0, 0.0)], axis=1).astype(BF16)
    spread = lax.broadcasted_iota(jnp.int32, (slots, slots * strip), 1) // strip == lax.broadcasted_iota(
        jnp.int32, (slots, slots * strip), 0
    )
    named = jnp.broadcast_to(routes[...].astype(F32), (8, slots)).astype(BF16)
    named = jnp.dot(named, jnp.where(spread, 1.0, 0.0).astype(BF16), preferred_element_type=F32)[0:1].astype(jnp.int32)
    shape = (32 * pair_rows, slots * strip)
    row = lax.broadcasted_iota(jnp.int32, shape, 0)
    col = lax.broadcasted_iota(jnp.int32, shape, 1)
    place, plane = row // (2 * pair_rows), 2 * ((row // strip) % 2) + (row // pair_rows) % 2
    factor = (place // 4) * 16 + plane * 4 + place % 4
    pick = jnp.where((named == factor) & (row % strip == col % strip), 1.0, 0.0).astype(BF16)
    chosen[...] = jnp.dot(pick, ext[...], preferred_element_type=F32).astype(BF16).reshape(32, pair_rows, wide)
    pl.semaphore_wait(barrier, jnp.where(even, 37, 39))

    def plane_copy(step, there):
        px, py = peer(*STEPS[step])
        return pltpu.make_async_remote_copy(
            chosen.at[2 * (px * 4 + py) + there],
            staged.at[2 * step + core],
            plane_send.at[step, there],
            plane_recv.at[step, core],
            device_id=device(z, there, px, py),
            device_id_type=MESH,
        )

    def plane_each(step, act):
        for there in range(2):
            if step > 0:
                act(plane_copy(step, there))
            else:

                @pl.when(core != there)
                def _():
                    act(plane_copy(step, there))

    def plane_wait(step):
        for source in range(2):
            landed = staged.at[2 * step + source]
            if step > 0:
                pltpu.make_async_copy(landed, landed, plane_recv.at[step, source]).wait()
            else:

                @pl.when(core != source)
                def _():
                    pltpu.make_async_copy(landed, landed, plane_recv.at[step, source]).wait()

    for step in range(16):
        plane_each(step, lambda copy: copy.start())
    staged[core] = chosen[2 * (x * 4 + y) + core]

    def origin(step):
        dx, dy = STEPS[step]
        return peer(4 - dx, 4 - dy)

    def direct(step):
        sx, sy = origin(step)
        return lax.rem(sx + sy, 2) == core

    def z_copy(step, dz, slot, near=False):
        sx, sy = origin(step)
        target = lax.rem(z + dz, 8)
        cell = cells.at[2 * step + lax.div(lax.rem(target, 4), 2)]
        landing = stack.at[step * 8 + z]
        if near:
            return pltpu.make_async_copy(cell, landing, group_recv.at[step])
        return pltpu.make_async_remote_copy(
            cell,
            landing,
            z_send.at[step, slot],
            group_recv.at[step],
            device_id=device(target, lax.rem(sx + sy, 2), x, y),
            device_id_type=MESH,
        )

    def z_start(step):
        plane_wait(step)
        one, two = staged[2 * step].astype(F32), staged[2 * step + 1].astype(F32)
        for j in range(2):
            part = slice(j * strip, (j + 1) * strip)
            cells[2 * step + j] = jnp.concatenate([one[part], two[part]], 0).astype(BF16)

        @pl.when(even)
        def _():
            for slot, dz in enumerate((4, 2, 6)):
                z_copy(step, dz, slot).start()

            @pl.when(direct(step))
            def _():
                z_copy(step, 0, 3, near=True).start()

            @pl.when(jnp.logical_not(direct(step)))
            def _():
                z_copy(step, 0, 3).start()

        @pl.when(jnp.logical_not(even))
        def _():
            for slot, dz in enumerate((5, 3, 1, 7)):
                z_copy(step, dz, slot).start()

    def z_finish(step):
        for slot in range(3):
            z_copy(step, 1, slot).wait_send()

        @pl.when(jnp.logical_not(even & direct(step)))
        def _():
            z_copy(step, 1, 3).wait_send()

    sibling = device(z, 1 - core, x, y)

    def pass_copy(step):
        group = stack.at[pl.ds(step * 8, 8)]
        return pltpu.make_async_remote_copy(
            group, group, pass_send.at[step], pass_recv.at[step], device_id=sibling, device_id_type=MESH
        )

    def arrive(pair):
        for step in (2 * pair, 2 * pair + 1):
            group = stack.at[pl.ds(step * 8, 8)]

            @pl.when(direct(step))
            def _():
                pltpu.make_async_copy(group, group, group_recv.at[step]).wait()
                pass_copy(step).start()

        for step in (2 * pair, 2 * pair + 1):

            @pl.when(jnp.logical_not(direct(step)))
            def _():
                pass_copy(step).wait_recv()

    depth, half = 16 * pair_rows, wide // 2

    def accumulate(pair):
        def body(i, _):
            at = pl.ds(pl.multiple_of(i * half, LANES), half)
            left = stack[pl.ds(pair * 16, 16), :, at].reshape(depth, half)
            block = stack[pl.ds(pair * 16, 16)].reshape(depth, wide)
            term = lax.dot_general(left, block, (((0,), (0,)), ((), ())), preferred_element_type=F32)
            if pair == 0:
                gram[at, :] = term
            else:
                gram[at, :] += term
            return 0

        lax.fori_loop(0, 2, body, 0)

    for turn in range(8 + LAG // 2):
        if turn < 8:
            z_start(2 * turn)
            z_start(2 * turn + 1)
        if turn >= LAG // 2:
            arrive(turn - LAG // 2)
            accumulate(turn - LAG // 2)

    eye = (
        lax.broadcasted_iota(jnp.int32, (LANES, LANES), 0) == lax.broadcasted_iota(jnp.int32, (LANES, LANES), 1)
    ).astype(F32)
    inside = lax.broadcasted_iota(jnp.int32, (1, LANES), 1) < width - last
    lane = lax.broadcasted_iota(jnp.int32, (1, LANES), 1)
    count = jnp.sum(jnp.where(lane == width - last, gram[pl.ds(width, 8), pl.ds(last, LANES)][0:1], 0.0))

    def clear(i, _):
        at = pl.ds(pl.multiple_of(i * TILE, TILE), TILE)
        gram[at, pl.ds(last, LANES)] = jnp.where(inside, gram[at, pl.ds(last, LANES)], 0.0)
        return 0

    lax.fori_loop(0, tiles, clear, 0)
    gram[pl.ds(width, wide - width), :] = jnp.zeros((wide - width, wide), F32)
    diagonal = jnp.zeros((LANES, LANES), F32)
    for b in range(wide // LANES):
        diagonal += gram[b * LANES : (b + 1) * LANES, b * LANES : (b + 1) * LANES] * eye
    trace = jnp.sum(diagonal)
    lift = damping[0] * trace / width
    stats[0, 0] = trace
    stats[0, 1] = count
    for b in range(wide // LANES):
        at = slice(b * LANES, (b + 1) * LANES)
        gram[at, at] += lift * (eye if b < wide // LANES - 1 else jnp.where(inside, eye, 0.0))

    for step in range(16):
        plane_each(step, lambda copy: copy.wait_send())
        z_finish(step)

        @pl.when(direct(step))
        def _():
            pass_copy(step).wait_send()


def invert(width, gram, stats, out, scale, t_all, t_rows, a_rows, t_next, vectors):
    member = lax.axis_index("grp")
    wide, rows = gram.shape[1], out.shape[0]
    last = wide - LANES

    blocks = wide // LANES
    trace = stats[0, 0]
    unit = width / trace
    eye = (
        lax.broadcasted_iota(jnp.int32, (LANES, LANES), 0) == lax.broadcasted_iota(jnp.int32, (LANES, LANES), 1)
    ).astype(F32)
    inside = lax.broadcasted_iota(jnp.int32, (1, LANES), 1) < width - last

    def multiply(_, carry):
        factors = [vectors[1, :, b * LANES : (b + 1) * LANES] for b in range(blocks)]
        vectors[0] = vectors[1]
        for i in range(blocks):
            parts = []
            for q in range(LANES // 8):
                at = slice(i * LANES + q * 8, i * LANES + q * 8 + 8)
                total = gram[at, :LANES] * factors[0]
                for b in range(1, blocks):
                    total += gram[at, b * LANES : (b + 1) * LANES] * factors[b]
                parts.append(total)
            total = jnp.sum(jnp.concatenate(parts, axis=0).T, axis=0, keepdims=True) * unit
            vectors[1, :, i * LANES : (i + 1) * LANES] = jnp.broadcast_to(total, (8, LANES))
        return carry

    def half_turns(_, carry):
        lax.fori_loop(0, POWER // 2, multiply, 0)
        size = lax.rsqrt(jnp.sum(vectors[1] * vectors[1]) * 0.125)
        vectors[...] = vectors[...] * size
        return carry

    lane_all = lax.broadcasted_iota(jnp.int32, (8, wide), 1)
    vectors[1] = jnp.where(lane_all < width, 1.0 / math.sqrt(width), 0.0).astype(F32)
    lax.fori_loop(0, 2, half_turns, 0)
    before, vector = vectors[0], vectors[1]
    bound = 1.1 * (jnp.sum(before * vector) / jnp.sum(before * before))
    scale[0, 0] = bound * (trace / (stats[0, 1] * width))
    rate = unit / bound

    def normalize(i, _):
        at = pl.ds(pl.multiple_of(i * LANES, LANES), LANES)
        t_all[at, :] = (gram[at, :] * (-0.5 * rate)).astype(BF16)
        return 0

    lax.fori_loop(0, blocks, normalize, 0)
    parts = []
    for b in range(blocks):
        at = slice(b * LANES, (b + 1) * LANES)
        ones = eye if b < blocks - 1 else jnp.where(inside, eye, 0.0)
        y_part = (gram[at, at] * rate).astype(BF16).astype(F32)
        t_part = ((3.0 * ones - y_part) * 0.5).astype(BF16)
        t_all[at, at] = t_part
        parts.append(jnp.sum((y_part + 2.0 * t_part.astype(F32)) * eye, axis=0, keepdims=True))
    lift_back = jnp.concatenate(parts, axis=1)

    first = member * rows
    t_rows[...] = t_all[pl.ds(pl.multiple_of(first, 16), rows), :]
    square = jnp.dot(t_rows[...], t_all[...], preferred_element_type=F32)
    a_rows[...] = (t_rows[...].astype(F32) * lift_back - 2.0 * square).astype(BF16)
    m_rows = jnp.dot(a_rows[...], t_all[...], preferred_element_type=F32)
    row = lax.broadcasted_iota(jnp.int32, (rows, wide), 0) + first
    col = lax.broadcasted_iota(jnp.int32, (rows, wide), 1)
    t_next[...] = (jnp.where(row == col, 1.5, 0.0) - 0.5 * m_rows).astype(BF16)
    out[...] = jnp.dot(t_next[...], t_all[...], preferred_element_type=F32)[:, :width]


def invert_call(gram, stats, width, rows):
    wide = gram.shape[1]
    vmem = pl.BlockSpec(memory_space=pltpu.VMEM)
    smem = pl.BlockSpec(memory_space=pltpu.SMEM)
    return pl.pallas_call(
        functools.partial(invert, width),
        out_shape=(jax.ShapeDtypeStruct((rows, width), F32), jax.ShapeDtypeStruct((1, 1), F32)),
        in_specs=[vmem, smem],
        out_specs=(vmem, smem),
        scratch_shapes=[
            pltpu.VMEM((wide, wide), BF16),
            pltpu.VMEM((rows, wide), BF16),
            pltpu.VMEM((rows, wide), BF16),
            pltpu.VMEM((rows, wide), BF16),
            pltpu.VMEM((2, 8, wide), F32),
        ],
        compiler_params=pltpu.CompilerParams(vmem_limit_bytes=36 * 1024 * 1024),
        name="invert",
    )(gram, stats)


def per_device(samples, routes, damping):
    members = lax.axis_size("grp")
    _, slots, strip, width = samples.shape
    wide = -(-width // TILE) * TILE
    rows = width // members
    vmem = pl.BlockSpec(memory_space=pltpu.VMEM)
    smem = pl.BlockSpec(memory_space=pltpu.SMEM)
    dma = pltpu.SemaphoreType.DMA
    gram, stats = pl.pallas_call(
        functools.partial(collect, width, strip, slots),
        out_shape=(pltpu.VMEM((wide, wide), F32), jax.ShapeDtypeStruct((1, 2), F32)),
        in_specs=[vmem, vmem, smem],
        out_specs=(vmem, smem),
        scratch_shapes=[
            pltpu.VMEM((slots * strip, wide), BF16),
            pltpu.VMEM((32, 2 * strip, wide), BF16),
            pltpu.VMEM((32, 2 * strip, wide), BF16),
            pltpu.VMEM((32, 2 * strip, wide), BF16),
            pltpu.VMEM((128, 2 * strip, wide), BF16),
            dma((16, 2)),
            dma((16, 2)),
            dma((16, 4)),
            dma((16,)),
            dma((16,)),
            dma((16,)),
        ],
        compiler_params=pltpu.CompilerParams(
            collective_id=0, has_side_effects=True, vmem_limit_bytes=26 * 1024 * 1024
        ),
        name="collect",
    )(samples.reshape(slots * strip, width), routes.reshape(1, slots), damping)
    result, scale = invert_call(gram, stats, width, rows)
    return (result[None], scale.reshape(1))


def solution(mesh):
    in_specs = (P("grp", "wide", None, None), P("grp", "wide", None), P("wide"))
    out_specs = (P("wide", "grp", None), P("wide"))
    return jax.shard_map(
        per_device, mesh=mesh, in_specs=in_specs, out_specs=out_specs, check_vma=False
    )
```

```python
import functools
import math

import jax
import jax.numpy as jnp
from jax import lax
from jax.experimental import pallas as pl
from jax.experimental.pallas import tpu as pltpu
from jax.sharding import PartitionSpec as P

POWER = 6
MESH = pl.DeviceIdType.MESH
F32, BF16 = jnp.float32, jnp.bfloat16
LANES = 128
TILE = 256

STEPS = (
    (0, 0), (1, 0), (1, 1), (3, 0), (3, 3), (0, 1), (1, 3), (0, 3),
    (3, 1), (2, 1), (2, 0), (1, 2), (0, 2), (2, 3), (2, 2), (3, 2),
)
LAG = 6


def device(z, core, x, y):
    return (lax.div(z, 4) * 2 + core, x * 16 + lax.rem(z, 4) * 4 + y)


def collect(width, strip, slots, strips_hbm, routes_hbm, damping, gram, stats, strips, routes, ext, chosen, staged, cells, ends, held, flags, stack, strays, load_sem, plane_send, plane_recv, z_send, group_recv, pass_send, pass_recv, end_send, end_recv, over_send, over_recv):
    member, worker = lax.axis_index("grp"), lax.axis_index("wide")
    core = lax.rem(member, 2)
    x, y = lax.div(worker, 16), lax.rem(worker, 4)
    z = lax.div(member, 2) * 4 + lax.rem(lax.div(worker, 4), 4)
    even = lax.rem(z, 2) == core
    wide = ext.shape[1]
    pair_rows = 2 * strip
    last = wide - LANES

    def peer(dx, dy):
        return lax.rem(x + dx, 4), lax.rem(y + dy, 4)

    loads = [
        pltpu.make_async_copy(strips_hbm, strips, load_sem.at[0]),
        pltpu.make_async_copy(routes_hbm, routes, load_sem.at[1]),
    ]
    for load in loads:
        load.start()

    barrier = pltpu.get_barrier_semaphore()
    pl.semaphore_signal(barrier, inc=1, device_id=device(z, 1 - core, x, y), device_id_type=MESH)
    for dx, dy in STEPS[1:]:
        px, py = peer(dx, dy)
        for there in range(2):
            pl.semaphore_signal(barrier, inc=1, device_id=device(z, there, px, py), device_id_type=MESH)
    for dz in range(1, 8):
        pl.semaphore_signal(barrier, inc=1, device_id=device(lax.rem(z + dz, 8), lax.rem(z, 2), x, y), device_id_type=MESH)

    for load in loads:
        load.wait()
    ext[:, :last] = strips[:, :last]
    mark = lax.broadcasted_iota(jnp.int32, (slots * strip, wide - width), 1) == 0
    ext[:, last:] = jnp.concatenate([strips[:, last:].astype(F32), jnp.where(mark, 1.0, 0.0)], axis=1).astype(BF16)
    spread = lax.broadcasted_iota(jnp.int32, (slots, slots * strip), 1) // strip == lax.broadcasted_iota(
        jnp.int32, (slots, slots * strip), 0
    )
    named = jnp.broadcast_to(routes[...].astype(F32), (8, slots)).astype(BF16)
    named = jnp.dot(named, jnp.where(spread, 1.0, 0.0).astype(BF16), preferred_element_type=F32)[0:1].astype(jnp.int32)
    shape = (32 * pair_rows, slots * strip)
    row = lax.broadcasted_iota(jnp.int32, shape, 0)
    col = lax.broadcasted_iota(jnp.int32, shape, 1)
    place, plane = row // (2 * pair_rows), 2 * ((row // strip) % 2) + (row // pair_rows) % 2
    factor = (place // 4) * 16 + plane * 4 + place % 4
    pick = jnp.where((named == factor) & (row % strip == col % strip), 1.0, 0.0).astype(BF16)
    chosen[...] = jnp.dot(pick, ext[...], preferred_element_type=F32).astype(BF16).reshape(32, pair_rows, wide)
    pl.semaphore_wait(barrier, jnp.where(even, 37, 39))

    def plane_copy(step, there):
        px, py = peer(*STEPS[step])
        return pltpu.make_async_remote_copy(
            chosen.at[2 * (px * 4 + py) + there],
            staged.at[2 * step + core],
            plane_send.at[step, there],
            plane_recv.at[step, core],
            device_id=device(z, there, px, py),
            device_id_type=MESH,
        )

    def plane_each(step, act):
        for there in range(2):
            if step > 0:
                act(plane_copy(step, there))
            else:

                @pl.when(core != there)
                def _():
                    act(plane_copy(step, there))

    def plane_wait(step):
        for source in range(2):
            landed = staged.at[2 * step + source]
            if step > 0:
                pltpu.make_async_copy(landed, landed, plane_recv.at[step, source]).wait()
            else:

                @pl.when(core != source)
                def _():
                    pltpu.make_async_copy(landed, landed, plane_recv.at[step, source]).wait()

    for step in range(16):
        plane_each(step, lambda copy: copy.start())
    staged[core] = chosen[2 * (x * 4 + y) + core]

    def origin(step):
        dx, dy = STEPS[step]
        return peer(4 - dx, 4 - dy)

    def direct(step):
        sx, sy = origin(step)
        return lax.rem(sx + sy, 2) == core

    def end_step(entry):
        return 4 * (entry // 2) + 2 + entry % 2 if entry < 8 else 15

    def z_copy(step, dz, slot, near=False, entry=None):
        sx, sy = origin(step)
        target = lax.rem(z + dz, 8)
        j = lax.div(lax.rem(target, 4), 2)
        if entry is None:
            source, landing = cells.at[2 * step + j], stack.at[step * 8 + z]
            sent, landed = z_send.at[step, slot], group_recv.at[step]
        else:
            source, landing = ends.at[2 * entry + j], strays.at[entry * 8 + z]
            sent, landed = end_send.at[entry, slot], end_recv.at[entry]
        if near:
            return pltpu.make_async_copy(source, landing, landed)
        return pltpu.make_async_remote_copy(
            source,
            landing,
            sent,
            landed,
            device_id=device(target, lax.rem(sx + sy, 2), x, y),
            device_id_type=MESH,
        )

    def z_spread(step, entry=None):
        @pl.when(even)
        def _():
            for slot, dz in enumerate((4, 2, 6)):
                z_copy(step, dz, slot, entry=entry).start()

            @pl.when(direct(step))
            def _():
                z_copy(step, 0, 3, near=True, entry=entry).start()

            @pl.when(jnp.logical_not(direct(step)))
            def _():
                z_copy(step, 0, 3, entry=entry).start()

        @pl.when(jnp.logical_not(even))
        def _():
            for slot, dz in enumerate((5, 3, 1, 7)):
                z_copy(step, dz, slot, entry=entry).start()

    def z_start(step):
        plane_wait(step)
        one, two = staged[2 * step].astype(F32), staged[2 * step + 1].astype(F32)
        for j in range(2):
            part = slice(j * strip, (j + 1) * strip)
            cell = jnp.concatenate([one[part], two[part]], 0)
            cells[2 * step + j] = cell[:, :last].astype(BF16)
            end = cell[:, last:]
            flags[j] = end if step == 0 else flags[j] + end
            if step % 4 < 2:
                held[2 * (step % 2) + j] = end
            else:
                entry = 2 * (step // 4) + step % 2
                former = held[2 * (step % 2) + j]
                ends[2 * entry + j] = jnp.concatenate([former[:, : width - last], end[:, : width - last]], 1).astype(BF16)
        z_spread(step)
        if step % 4 >= 2:
            z_spread(step, 2 * (step // 4) + step % 2)
        if step == 15:
            lane = lax.broadcasted_iota(jnp.int32, (pair_rows, LANES), 1)
            for j in range(2):
                total = jnp.sum(jnp.where(lane == width - last, flags[j], 0.0))
                ends[16 + j] = jnp.broadcast_to(total, (pair_rows, LANES)).astype(BF16)
            z_spread(step, 8)

    def z_finish(step, entry=None):
        for slot in range(3):
            z_copy(step, 1, slot, entry=entry).wait_send()

        @pl.when(jnp.logical_not(even & direct(step)))
        def _():
            z_copy(step, 1, 3, entry=entry).wait_send()

    sibling = device(z, 1 - core, x, y)

    def pass_copy(step, entry=None):
        if entry is None:
            group, sent, landed = stack.at[pl.ds(step * 8, 8)], pass_send.at[step], pass_recv.at[step]
        else:
            group, sent, landed = strays.at[pl.ds(entry * 8, 8)], over_send.at[entry], over_recv.at[entry]
        return pltpu.make_async_remote_copy(
            group, group, sent, landed, device_id=sibling, device_id_type=MESH
        )

    def arrive(step, entry=None):
        if entry is None:
            group, landed = stack.at[pl.ds(step * 8, 8)], group_recv.at[step]
        else:
            group, landed = strays.at[pl.ds(entry * 8, 8)], end_recv.at[entry]

        @pl.when(direct(step))
        def _():
            pltpu.make_async_copy(group, group, landed).wait()
            pass_copy(step, entry).start()

    def passed(step, entry=None):
        @pl.when(jnp.logical_not(direct(step)))
        def _():
            pass_copy(step, entry).wait_recv()

    def pass_finish(step, entry=None):
        @pl.when(direct(step))
        def _():
            pass_copy(step, entry).wait_send()

    depth, middle = 16 * pair_rows, wide // 2

    def accumulate(pair):
        for start, stop in ((0, middle), (middle, last)):
            left = stack[pl.ds(pair * 16, 16), :, start:stop].reshape(depth, stop - start)
            block = stack[pl.ds(pair * 16, 16)].reshape(depth, last)
            term = lax.dot_general(left, block, (((0,), (0,)), ((), ())), preferred_element_type=F32)
            if pair == 0:
                gram[start:stop, :last] = term
            else:
                gram[start:stop, :last] += term

    def accumulate_ends(quad):
        blank = jnp.zeros((8 * pair_rows, wide - width), F32)
        parts = []
        for i in range(4):
            pair_of = strays[pl.ds((2 * quad + i % 2) * 8, 8)].reshape(8 * pair_rows, LANES).astype(F32)
            kept = pair_of[:, : width - last] if i < 2 else pair_of[:, width - last :]
            parts.append(jnp.concatenate([kept, blank], 1))
        left = jnp.concatenate(parts, 0).astype(BF16)
        block = stack[pl.ds(quad * 32, 32)].reshape(2 * depth, last)
        for where, right in ((slice(0, last), block), (slice(last, wide), left)):
            term = lax.dot_general(left, right, (((0,), (0,)), ((), ())), preferred_element_type=F32)
            if quad == 0:
                gram[last:, where] = term
            else:
                gram[last:, where] += term

    def entries(pair):
        return [entry for entry in range(9) if end_step(entry) // 2 == pair]

    for turn in range(8 + LAG // 2):
        if turn < 8:
            z_start(2 * turn)
            z_start(2 * turn + 1)
        if turn >= LAG // 2:
            pair = turn - LAG // 2
            items = [(step, None) for step in (2 * pair, 2 * pair + 1)]
            items += [(end_step(entry), entry) for entry in entries(pair)]
            for item in items:
                arrive(*item)
            if turn == 8:
                for step in range(16):
                    plane_each(step, lambda copy: copy.wait_send())
            done = {8: range(4), 9: range(4, 6), 10: range(6, 8)}.get(turn, ())
            for other in done:
                for item in [(step, None) for step in (2 * other, 2 * other + 1)]:
                    z_finish(*item)
                for entry in entries(other):
                    z_finish(end_step(entry), entry)
                if other < 7:
                    for item in [(step, None) for step in (2 * other, 2 * other + 1)]:
                        pass_finish(*item)
                    for entry in entries(other):
                        pass_finish(end_step(entry), entry)
            for item in items:
                passed(*item)
            accumulate(pair)
            if pair % 2:
                accumulate_ends(pair // 2)
    for item in items:
        pass_finish(*item)

    for b in range(last // LANES):
        gram[b * LANES : (b + 1) * LANES, last:] = gram[last:, b * LANES : (b + 1) * LANES].T
    eye = (
        lax.broadcasted_iota(jnp.int32, (LANES, LANES), 0) == lax.broadcasted_iota(jnp.int32, (LANES, LANES), 1)
    ).astype(F32)
    inside = lax.broadcasted_iota(jnp.int32, (1, LANES), 1) < width - last
    count = jnp.sum(strays[64:].astype(F32)) * (1.0 / (pair_rows * LANES))
    diagonal = jnp.zeros((LANES, LANES), F32)
    for b in range(wide // LANES):
        diagonal += gram[b * LANES : (b + 1) * LANES, b * LANES : (b + 1) * LANES] * eye
    trace = jnp.sum(diagonal)
    lift = damping[0] * trace / width
    stats[0, 0] = trace
    stats[0, 1] = count
    for b in range(wide // LANES):
        at = slice(b * LANES, (b + 1) * LANES)
        gram[at, at] += lift * (eye if b < wide // LANES - 1 else jnp.where(inside, eye, 0.0))


def invert(width, gram, stats, out, scale, t_all, t_rows, a_rows, t_next, vectors):
    wide, rows = gram.shape[1], out.shape[0]
    half = out.shape[1]
    last = wide - LANES
    first = lax.axis_index("grp") * rows

    @pl.when(pl.program_id(0) == 0)
    def _():
        blocks = wide // LANES
        trace = stats[0, 0]
        unit = width / trace
        eye = (
            lax.broadcasted_iota(jnp.int32, (LANES, LANES), 0) == lax.broadcasted_iota(jnp.int32, (LANES, LANES), 1)
        ).astype(F32)
        inside = lax.broadcasted_iota(jnp.int32, (1, LANES), 1) < width - last

        def multiply(_, carry):
            factors = [vectors[1, :, b * LANES : (b + 1) * LANES] for b in range(blocks)]
            vectors[0] = vectors[1]
            for i in range(blocks):
                parts = []
                for q in range(LANES // 8):
                    at = slice(i * LANES + q * 8, i * LANES + q * 8 + 8)
                    total = gram[at, :LANES] * factors[0]
                    for b in range(1, blocks):
                        total += gram[at, b * LANES : (b + 1) * LANES] * factors[b]
                    parts.append(total)
                total = jnp.sum(jnp.concatenate(parts, axis=0).T, axis=0, keepdims=True) * unit
                vectors[1, :, i * LANES : (i + 1) * LANES] = jnp.broadcast_to(total, (8, LANES))
            return carry

        def half_turns(_, carry):
            lax.fori_loop(0, POWER // 2, multiply, 0)
            size = lax.rsqrt(jnp.sum(vectors[1] * vectors[1]) * 0.125)
            vectors[...] = vectors[...] * size
            return carry

        lane_all = lax.broadcasted_iota(jnp.int32, (8, wide), 1)
        vectors[1] = jnp.where(lane_all < width, 1.0 / math.sqrt(width), 0.0).astype(F32)
        lax.fori_loop(0, 2, half_turns, 0)
        before, vector = vectors[0], vectors[1]
        bound = 1.1 * (jnp.sum(before * vector) / jnp.sum(before * before))
        scale[0, 0] = bound * (trace / (stats[0, 1] * width))
        rate = unit / bound

        def normalize(i, _):
            at = pl.ds(pl.multiple_of(i * LANES, LANES), LANES)
            t_all[at, :] = (gram[at, :] * (-0.5 * rate)).astype(BF16)
            return 0

        lax.fori_loop(0, blocks, normalize, 0)
        parts = []
        for b in range(blocks):
            at = slice(b * LANES, (b + 1) * LANES)
            ones = eye if b < blocks - 1 else jnp.where(inside, eye, 0.0)
            y_part = (gram[at, at] * rate).astype(BF16).astype(F32)
            t_part = ((3.0 * ones - y_part) * 0.5).astype(BF16)
            t_all[at, at] = t_part
            parts.append(jnp.sum((y_part + 2.0 * t_part.astype(F32)) * eye, axis=0, keepdims=True))
        lift_back = jnp.concatenate(parts, axis=1)

        t_rows[...] = t_all[pl.ds(pl.multiple_of(first, 16), rows), :]
        square = jnp.dot(t_rows[...], t_all[...], preferred_element_type=F32)
        a_rows[...] = (t_rows[...].astype(F32) * lift_back - 2.0 * square).astype(BF16)
        m_rows = jnp.dot(a_rows[...], t_all[...], preferred_element_type=F32)
        row = lax.broadcasted_iota(jnp.int32, (rows, wide), 0) + first
        col = lax.broadcasted_iota(jnp.int32, (rows, wide), 1)
        t_next[...] = (jnp.where(row == col, 1.5, 0.0) - 0.5 * m_rows).astype(BF16)
        out[...] = jnp.dot(t_next[...], t_all[:, :half], preferred_element_type=F32)

    @pl.when(pl.program_id(0) == 1)
    def _():
        out[...] = jnp.dot(t_next[...], t_all[:, half:], preferred_element_type=F32)


def invert_call(gram, stats, width, rows):
    wide = gram.shape[1]
    vmem = pl.BlockSpec(memory_space=pltpu.VMEM)
    smem = pl.BlockSpec(memory_space=pltpu.SMEM)
    return pl.pallas_call(
        functools.partial(invert, width),
        out_shape=(jax.ShapeDtypeStruct((rows, width), F32), jax.ShapeDtypeStruct((1, 1), F32)),
        grid=(2,),
        in_specs=[vmem, smem],
        out_specs=(pl.BlockSpec((rows, wide // 2), lambda i: (0, i)), smem),
        scratch_shapes=[
            pltpu.VMEM((wide, wide), BF16),
            pltpu.VMEM((rows, wide), BF16),
            pltpu.VMEM((rows, wide), BF16),
            pltpu.VMEM((rows, wide), BF16),
            pltpu.VMEM((2, 8, wide), F32),
        ],
        compiler_params=pltpu.CompilerParams(vmem_limit_bytes=36 * 1024 * 1024),
        name="invert",
    )(gram, stats)


def per_device(samples, routes, damping):
    members = lax.axis_size("grp")
    _, slots, strip, width = samples.shape
    wide = -(-width // TILE) * TILE
    rows = width // members
    vmem = pl.BlockSpec(memory_space=pltpu.VMEM)
    smem = pl.BlockSpec(memory_space=pltpu.SMEM)
    hbm = pl.BlockSpec(memory_space=pltpu.HBM)
    dma = pltpu.SemaphoreType.DMA
    gram, stats = pl.pallas_call(
        functools.partial(collect, width, strip, slots),
        out_shape=(pltpu.VMEM((wide, wide), F32), jax.ShapeDtypeStruct((1, 2), F32)),
        in_specs=[hbm, hbm, smem],
        out_specs=(vmem, smem),
        scratch_shapes=[
            pltpu.VMEM((slots * strip, width), BF16),
            pltpu.VMEM((1, slots), jnp.int32),
            pltpu.VMEM((slots * strip, wide), BF16),
            pltpu.VMEM((32, 2 * strip, wide), BF16),
            pltpu.VMEM((32, 2 * strip, wide), BF16),
            pltpu.VMEM((32, 2 * strip, wide - LANES), BF16),
            pltpu.VMEM((18, 2 * strip, LANES), BF16),
            pltpu.VMEM((4, 2 * strip, LANES), F32),
            pltpu.VMEM((2, 2 * strip, LANES), F32),
            pltpu.VMEM((128, 2 * strip, wide - LANES), BF16),
            pltpu.VMEM((72, 2 * strip, LANES), BF16),
            dma((2,)),
            dma((16, 2)),
            dma((16, 2)),
            dma((16, 4)),
            dma((16,)),
            dma((16,)),
            dma((16,)),
            dma((9, 4)),
            dma((9,)),
            dma((9,)),
            dma((9,)),
        ],
        compiler_params=pltpu.CompilerParams(
            collective_id=0, has_side_effects=True, vmem_limit_bytes=26 * 1024 * 1024
        ),
        name="collect",
    )(
        pltpu.with_memory_space_constraint(samples.reshape(slots * strip, width), pltpu.HBM),
        pltpu.with_memory_space_constraint(routes.reshape(1, slots), pltpu.HBM),
        damping,
    )
    result, scale = invert_call(gram, stats, width, rows)
    return (result[None], scale.reshape(1))


def solution(mesh):
    in_specs = (P("grp", "wide", None, None), P("grp", "wide", None), P("wide"))
    out_specs = (P("wide", "grp", None), P("wide"))
    return jax.shard_map(
        per_device, mesh=mesh, in_specs=in_specs, out_specs=out_specs, check_vma=False
    )
```

```python
import functools
import math

import jax
import jax.numpy as jnp
from jax import lax
from jax.experimental import pallas as pl
from jax.experimental.pallas import tpu as pltpu
from jax.sharding import PartitionSpec as P

POWER = 6
MESH = pl.DeviceIdType.MESH
F32, BF16 = jnp.float32, jnp.bfloat16
LANES = 128
TILE = 256

STEPS = (
    (0, 0), (1, 0), (1, 1), (3, 0), (3, 3), (0, 1), (1, 3), (0, 3),
    (3, 1), (2, 1), (2, 0), (1, 2), (0, 2), (2, 3), (2, 2), (3, 2),
)
LAG = 6


def device(z, core, x, y):
    return (lax.div(z, 4) * 2 + core, x * 16 + lax.rem(z, 4) * 4 + y)


def collect(width, strip, slots, strips_hbm, routes_hbm, damping, gram, stats, strips, routes, ext, chosen, staged, cells, ends, held, flags, stack, strays, load_sem, plane_send, plane_recv, z_send, group_recv, pass_send, pass_recv, end_send, end_recv, over_send, over_recv):
    member, worker = lax.axis_index("grp"), lax.axis_index("wide")
    core = lax.rem(member, 2)
    x, y = lax.div(worker, 16), lax.rem(worker, 4)
    z = lax.div(member, 2) * 4 + lax.rem(lax.div(worker, 4), 4)
    even = lax.rem(z, 2) == core
    wide = ext.shape[1]
    pair_rows = 2 * strip
    last = wide - LANES

    def peer(dx, dy):
        return lax.rem(x + dx, 4), lax.rem(y + dy, 4)

    loads = [
        pltpu.make_async_copy(strips_hbm, strips, load_sem.at[0]),
        pltpu.make_async_copy(routes_hbm, routes, load_sem.at[1]),
    ]
    for load in loads:
        load.start()

    barrier = pltpu.get_barrier_semaphore()
    pl.semaphore_signal(barrier, inc=1, device_id=device(z, 1 - core, x, y), device_id_type=MESH)
    for dx, dy in STEPS[1:]:
        px, py = peer(dx, dy)
        for there in range(2):
            pl.semaphore_signal(barrier, inc=1, device_id=device(z, there, px, py), device_id_type=MESH)
    for dz in range(1, 8):
        pl.semaphore_signal(barrier, inc=1, device_id=device(lax.rem(z + dz, 8), lax.rem(z, 2), x, y), device_id_type=MESH)

    for load in loads:
        load.wait()
    ext[:, :last] = strips[:, :last]
    mark = lax.broadcasted_iota(jnp.int32, (slots * strip, wide - width), 1) == 0
    ext[:, last:] = jnp.concatenate([strips[:, last:].astype(F32), jnp.where(mark, 1.0, 0.0)], axis=1).astype(BF16)
    spread = lax.broadcasted_iota(jnp.int32, (slots, slots * strip), 1) // strip == lax.broadcasted_iota(
        jnp.int32, (slots, slots * strip), 0
    )
    named = jnp.broadcast_to(routes[...].astype(F32), (8, slots)).astype(BF16)
    named = jnp.dot(named, jnp.where(spread, 1.0, 0.0).astype(BF16), preferred_element_type=F32)[0:1].astype(jnp.int32)
    shape = (32 * pair_rows, slots * strip)
    row = lax.broadcasted_iota(jnp.int32, shape, 0)
    col = lax.broadcasted_iota(jnp.int32, shape, 1)
    place, plane = row // (2 * pair_rows), 2 * ((row // strip) % 2) + (row // pair_rows) % 2
    factor = (place // 4) * 16 + plane * 4 + place % 4
    pick = jnp.where((named == factor) & (row % strip == col % strip), 1.0, 0.0).astype(BF16)
    chosen[...] = jnp.dot(pick, ext[...], preferred_element_type=F32).astype(BF16).reshape(32, pair_rows, wide)
    pl.semaphore_wait(barrier, jnp.where(even, 37, 39))

    def plane_copy(step, there):
        px, py = peer(*STEPS[step])
        return pltpu.make_async_remote_copy(
            chosen.at[2 * (px * 4 + py) + there],
            staged.at[2 * step + core],
            plane_send.at[step, there],
            plane_recv.at[step, core],
            device_id=device(z, there, px, py),
            device_id_type=MESH,
        )

    def plane_each(step, act):
        for there in range(2):
            if step > 0:
                act(plane_copy(step, there))
            else:

                @pl.when(core != there)
                def _():
                    act(plane_copy(step, there))

    def plane_wait(step):
        for source in range(2):
            landed = staged.at[2 * step + source]
            if step > 0:
                pltpu.make_async_copy(landed, landed, plane_recv.at[step, source]).wait()
            else:

                @pl.when(core != source)
                def _():
                    pltpu.make_async_copy(landed, landed, plane_recv.at[step, source]).wait()

    for step in range(16):
        plane_each(step, lambda copy: copy.start())
    staged[core] = chosen[2 * (x * 4 + y) + core]

    def origin(step):
        dx, dy = STEPS[step]
        return peer(4 - dx, 4 - dy)

    def direct(step):
        sx, sy = origin(step)
        return lax.rem(sx + sy, 2) == core

    def end_step(entry):
        return 4 * (entry // 2) + 2 + entry % 2 if entry < 8 else 15

    def z_copy(step, dz, slot, near=False, entry=None):
        sx, sy = origin(step)
        target = lax.rem(z + dz, 8)
        j = lax.div(lax.rem(target, 4), 2)
        if entry is None:
            source, landing = cells.at[2 * step + j], stack.at[step * 8 + z]
            sent, landed = z_send.at[step, slot], group_recv.at[step]
        else:
            source, landing = ends.at[2 * entry + j], strays.at[entry * 8 + z]
            sent, landed = end_send.at[entry, slot], end_recv.at[entry]
        if near:
            return pltpu.make_async_copy(source, landing, landed)
        return pltpu.make_async_remote_copy(
            source,
            landing,
            sent,
            landed,
            device_id=device(target, lax.rem(sx + sy, 2), x, y),
            device_id_type=MESH,
        )

    def z_spread(step, entry=None):
        @pl.when(even)
        def _():
            for slot, dz in enumerate((4, 2, 6)):
                z_copy(step, dz, slot, entry=entry).start()

            @pl.when(direct(step))
            def _():
                z_copy(step, 0, 3, near=True, entry=entry).start()

            @pl.when(jnp.logical_not(direct(step)))
            def _():
                z_copy(step, 0, 3, entry=entry).start()

        @pl.when(jnp.logical_not(even))
        def _():
            for slot, dz in enumerate((5, 3, 1, 7)):
                z_copy(step, dz, slot, entry=entry).start()

    def z_start(step):
        plane_wait(step)
        one, two = staged[2 * step].astype(F32), staged[2 * step + 1].astype(F32)
        for j in range(2):
            part = slice(j * strip, (j + 1) * strip)
            cell = jnp.concatenate([one[part], two[part]], 0)
            cells[2 * step + j] = cell[:, :last].astype(BF16)
            end = cell[:, last:]
            flags[j] = end if step == 0 else flags[j] + end
            if step % 4 < 2:
                held[2 * (step % 2) + j] = end
            else:
                entry = 2 * (step // 4) + step % 2
                former = held[2 * (step % 2) + j]
                ends[2 * entry + j] = jnp.concatenate([former[:, : width - last], end[:, : width - last]], 1).astype(BF16)
        z_spread(step)
        if step % 4 >= 2:
            z_spread(step, 2 * (step // 4) + step % 2)
        if step == 15:
            lane = lax.broadcasted_iota(jnp.int32, (pair_rows, LANES), 1)
            for j in range(2):
                total = jnp.sum(jnp.where(lane == width - last, flags[j], 0.0))
                ends[16 + j] = jnp.broadcast_to(total, (pair_rows, LANES)).astype(BF16)
            z_spread(step, 8)

    def z_finish(step, entry=None):
        for slot in range(3):
            z_copy(step, 1, slot, entry=entry).wait_send()

        @pl.when(jnp.logical_not(even & direct(step)))
        def _():
            z_copy(step, 1, 3, entry=entry).wait_send()

    sibling = device(z, 1 - core, x, y)

    def pass_copy(step, entry=None):
        if entry is None:
            group, sent, landed = stack.at[pl.ds(step * 8, 8)], pass_send.at[step], pass_recv.at[step]
        else:
            group, sent, landed = strays.at[pl.ds(entry * 8, 8)], over_send.at[entry], over_recv.at[entry]
        return pltpu.make_async_remote_copy(
            group, group, sent, landed, device_id=sibling, device_id_type=MESH
        )

    def arrive(step, entry=None):
        if entry is None:
            group, landed = stack.at[pl.ds(step * 8, 8)], group_recv.at[step]
        else:
            group, landed = strays.at[pl.ds(entry * 8, 8)], end_recv.at[entry]

        @pl.when(direct(step))
        def _():
            pltpu.make_async_copy(group, group, landed).wait()
            pass_copy(step, entry).start()

    def passed(step, entry=None):
        @pl.when(jnp.logical_not(direct(step)))
        def _():
            pass_copy(step, entry).wait_recv()

    def pass_finish(step, entry=None):
        @pl.when(direct(step))
        def _():
            pass_copy(step, entry).wait_send()

    depth, middle = 16 * pair_rows, wide // 2

    def accumulate(pair):
        for start, stop in ((0, middle), (middle, last)):
            left = stack[pl.ds(pair * 16, 16), :, start:stop].reshape(depth, stop - start)
            block = stack[pl.ds(pair * 16, 16)].reshape(depth, last)
            term = lax.dot_general(left, block, (((0,), (0,)), ((), ())), preferred_element_type=F32)
            if pair == 0:
                gram[start:stop, :last] = term
            else:
                gram[start:stop, :last] += term

    def accumulate_ends(quad):
        blank = jnp.zeros((8 * pair_rows, wide - width), F32)
        parts = []
        for i in range(4):
            pair_of = strays[pl.ds((2 * quad + i % 2) * 8, 8)].reshape(8 * pair_rows, LANES).astype(F32)
            kept = pair_of[:, : width - last] if i < 2 else pair_of[:, width - last :]
            parts.append(jnp.concatenate([kept, blank], 1))
        left = jnp.concatenate(parts, 0).astype(BF16)
        block = stack[pl.ds(quad * 32, 32)].reshape(2 * depth, last)
        for where, right in ((slice(0, last), block), (slice(last, wide), left)):
            term = lax.dot_general(left, right, (((0,), (0,)), ((), ())), preferred_element_type=F32)
            if quad == 0:
                gram[last:, where] = term
            else:
                gram[last:, where] += term

    def entries(pair):
        return [entry for entry in range(9) if end_step(entry) // 2 == pair]

    for turn in range(8 + LAG // 2):
        if turn < 8:
            z_start(2 * turn)
            z_start(2 * turn + 1)
        if turn >= LAG // 2:
            pair = turn - LAG // 2
            items = [(step, None) for step in (2 * pair, 2 * pair + 1)]
            items += [(end_step(entry), entry) for entry in entries(pair)]
            for item in items:
                arrive(*item)
            if turn == 8:
                for step in range(16):
                    plane_each(step, lambda copy: copy.wait_send())
            done = {8: range(4), 9: range(4, 6), 10: range(6, 8)}.get(turn, ())
            for other in done:
                for item in [(step, None) for step in (2 * other, 2 * other + 1)]:
                    z_finish(*item)
                for entry in entries(other):
                    z_finish(end_step(entry), entry)
                if other < 7:
                    for item in [(step, None) for step in (2 * other, 2 * other + 1)]:
                        pass_finish(*item)
                    for entry in entries(other):
                        pass_finish(end_step(entry), entry)
            for item in items:
                passed(*item)
            accumulate(pair)
            if pair % 2:
                accumulate_ends(pair // 2)
    for item in items:
        pass_finish(*item)

    for b in range(last // LANES):
        gram[b * LANES : (b + 1) * LANES, last:] = gram[last:, b * LANES : (b + 1) * LANES].T
    eye = (
        lax.broadcasted_iota(jnp.int32, (LANES, LANES), 0) == lax.broadcasted_iota(jnp.int32, (LANES, LANES), 1)
    ).astype(F32)
    inside = lax.broadcasted_iota(jnp.int32, (1, LANES), 1) < width - last
    count = jnp.sum(strays[64:].astype(F32)) * (1.0 / (pair_rows * LANES))
    diagonal = jnp.zeros((LANES, LANES), F32)
    for b in range(wide // LANES):
        diagonal += gram[b * LANES : (b + 1) * LANES, b * LANES : (b + 1) * LANES] * eye
    trace = jnp.sum(diagonal)
    lift = damping[0] * trace / width
    stats[0, 0] = trace
    stats[0, 1] = count
    for b in range(wide // LANES):
        at = slice(b * LANES, (b + 1) * LANES)
        gram[at, at] += lift * (eye if b < wide // LANES - 1 else jnp.where(inside, eye, 0.0))


def invert(width, gram, stats, out, scale, t_all, t_rows, a_rows, t_next, vectors):
    wide, rows = gram.shape[1], out.shape[0]
    share = out.shape[1]
    last = wide - LANES
    first = lax.axis_index("grp") * rows

    @pl.when(pl.program_id(0) == 0)
    def _():
        blocks = wide // LANES
        trace = stats[0, 0]
        unit = width / trace
        eye = (
            lax.broadcasted_iota(jnp.int32, (LANES, LANES), 0) == lax.broadcasted_iota(jnp.int32, (LANES, LANES), 1)
        ).astype(F32)
        inside = lax.broadcasted_iota(jnp.int32, (1, LANES), 1) < width - last

        def multiply(_, carry):
            factors = [vectors[1, :, b * LANES : (b + 1) * LANES] for b in range(blocks)]
            vectors[0] = vectors[1]
            for i in range(blocks):
                parts = []
                for q in range(LANES // 8):
                    at = slice(i * LANES + q * 8, i * LANES + q * 8 + 8)
                    total = gram[at, :LANES] * factors[0]
                    for b in range(1, blocks):
                        total += gram[at, b * LANES : (b + 1) * LANES] * factors[b]
                    parts.append(total)
                total = jnp.sum(jnp.concatenate(parts, axis=0).T, axis=0, keepdims=True) * unit
                vectors[1, :, i * LANES : (i + 1) * LANES] = jnp.broadcast_to(total, (8, LANES))
            return carry

        def half_turns(_, carry):
            lax.fori_loop(0, POWER // 2, multiply, 0)
            size = lax.rsqrt(jnp.sum(vectors[1] * vectors[1]) * 0.125)
            vectors[...] = vectors[...] * size
            return carry

        lane_all = lax.broadcasted_iota(jnp.int32, (8, wide), 1)
        vectors[1] = jnp.where(lane_all < width, 1.0 / math.sqrt(width), 0.0).astype(F32)
        lax.fori_loop(0, 2, half_turns, 0)
        before, vector = vectors[0], vectors[1]
        bound = 1.1 * (jnp.sum(before * vector) / jnp.sum(before * before))
        scale[0, 0] = bound * (trace / (stats[0, 1] * width))
        rate = unit / bound

        for i in range(blocks):
            at = slice(i * LANES, (i + 1) * LANES)
            t_all[at, :] = (gram[at, :] * (-0.5 * rate)).astype(BF16)
        parts = []
        for b in range(blocks):
            at = slice(b * LANES, (b + 1) * LANES)
            ones = eye if b < blocks - 1 else jnp.where(inside, eye, 0.0)
            y_part = (gram[at, at] * rate).astype(BF16).astype(F32)
            t_part = ((3.0 * ones - y_part) * 0.5).astype(BF16)
            t_all[at, at] = t_part
            parts.append(jnp.sum((y_part + 2.0 * t_part.astype(F32)) * eye, axis=0, keepdims=True))
        lift_back = jnp.concatenate(parts, axis=1)

        t_rows[...] = t_all[pl.ds(pl.multiple_of(first, 16), rows), :]
        square = jnp.dot(t_rows[...], t_all[...], preferred_element_type=F32)
        a_rows[...] = (t_rows[...].astype(F32) * lift_back - 2.0 * square).astype(BF16)
        m_rows = jnp.dot(a_rows[...], t_all[...], preferred_element_type=F32)
        row = lax.broadcasted_iota(jnp.int32, (rows, wide), 0) + first
        col = lax.broadcasted_iota(jnp.int32, (rows, wide), 1)
        t_next[...] = (jnp.where(row == col, 1.5, 0.0) - 0.5 * m_rows).astype(BF16)
        out[...] = jnp.dot(t_next[...], t_all[:, :share], preferred_element_type=F32)

    @pl.when(pl.program_id(0) == 1)
    def _():
        out[:, : wide - share] = jnp.dot(t_next[...], t_all[:, share:], preferred_element_type=F32)


def invert_call(gram, stats, width, rows):
    wide = gram.shape[1]
    share = -(-wide // (2 * TILE)) * TILE
    vmem = pl.BlockSpec(memory_space=pltpu.VMEM)
    smem = pl.BlockSpec(memory_space=pltpu.SMEM)
    return pl.pallas_call(
        functools.partial(invert, width),
        out_shape=(jax.ShapeDtypeStruct((rows, width), F32), jax.ShapeDtypeStruct((1, 1), F32)),
        grid=(2,),
        in_specs=[vmem, smem],
        out_specs=(pl.BlockSpec((rows, share), lambda i: (0, i)), smem),
        scratch_shapes=[
            pltpu.VMEM((wide, wide), BF16),
            pltpu.VMEM((rows, wide), BF16),
            pltpu.VMEM((rows, wide), BF16),
            pltpu.VMEM((rows, wide), BF16),
            pltpu.VMEM((2, 8, wide), F32),
        ],
        compiler_params=pltpu.CompilerParams(vmem_limit_bytes=36 * 1024 * 1024),
        name="invert",
    )(gram, stats)


def per_device(samples, routes, damping):
    members = lax.axis_size("grp")
    _, slots, strip, width = samples.shape
    wide = -(-width // TILE) * TILE
    rows = width // members
    vmem = pl.BlockSpec(memory_space=pltpu.VMEM)
    smem = pl.BlockSpec(memory_space=pltpu.SMEM)
    hbm = pl.BlockSpec(memory_space=pltpu.HBM)
    dma = pltpu.SemaphoreType.DMA
    gram, stats = pl.pallas_call(
        functools.partial(collect, width, strip, slots),
        out_shape=(pltpu.VMEM((wide, wide), F32), jax.ShapeDtypeStruct((1, 2), F32)),
        in_specs=[hbm, hbm, smem],
        out_specs=(vmem, smem),
        scratch_shapes=[
            pltpu.VMEM((slots * strip, width), BF16),
            pltpu.VMEM((1, slots), jnp.int32),
            pltpu.VMEM((slots * strip, wide), BF16),
            pltpu.VMEM((32, 2 * strip, wide), BF16),
            pltpu.VMEM((32, 2 * strip, wide), BF16),
            pltpu.VMEM((32, 2 * strip, wide - LANES), BF16),
            pltpu.VMEM((18, 2 * strip, LANES), BF16),
            pltpu.VMEM((4, 2 * strip, LANES), F32),
            pltpu.VMEM((2, 2 * strip, LANES), F32),
            pltpu.VMEM((128, 2 * strip, wide - LANES), BF16),
            pltpu.VMEM((72, 2 * strip, LANES), BF16),
            dma((2,)),
            dma((16, 2)),
            dma((16, 2)),
            dma((16, 4)),
            dma((16,)),
            dma((16,)),
            dma((16,)),
            dma((9, 4)),
            dma((9,)),
            dma((9,)),
            dma((9,)),
        ],
        compiler_params=pltpu.CompilerParams(
            collective_id=0, has_side_effects=True, vmem_limit_bytes=26 * 1024 * 1024
        ),
        name="collect",
    )(
        pltpu.with_memory_space_constraint(samples.reshape(slots * strip, width), pltpu.HBM),
        pltpu.with_memory_space_constraint(routes.reshape(1, slots), pltpu.HBM),
        damping,
    )
    result, scale = invert_call(gram, stats, width, rows)
    return (result[None], scale.reshape(1))


def solution(mesh):
    in_specs = (P("grp", "wide", None, None), P("grp", "wide", None), P("wide"))
    out_specs = (P("wide", "grp", None), P("wide"))
    return jax.shard_map(
        per_device, mesh=mesh, in_specs=in_specs, out_specs=out_specs, check_vma=False
    )
```
